32 devices in a mesh: seq: 16 (over z, y, x), head: 2 (over core).
Axes of the slice: x: 2, y: 2, z: 4, core: 2. Of those that a mesh axis runs over, the one named last changes fastest.
Arguments:
- queries: bfloat16 [4096, 4096], P('seq', 'head'), may hold values from -6 to 6
- keys: bfloat16 [4096, 4096], P('seq', 'head'), may hold values from -6 to 6
- values: bfloat16 [4096, 4096], P('seq', 'head'), may hold values from -6 to 6
- gain: float32 [4096], P('head'), may hold values from 0.1 to 1.9
- w_out: bfloat16 [4096, 3072], P('head', 'seq'), may hold values from -0.09375 to 0.09375
Outputs:
- mixed: bfloat16 [4096, 3072], P(('seq', 'head'))
The draws below stay inside these ranges and needn't reach their ends.
All inputs are finite; a program needn't handle non-finite values.
Results may differ from the reference program's by a relative error of at most 0.0049.
Values may be sent and summed in bfloat16 or wider, within the bound.
A program may use at most 320 MiB of HBM per device.

```python
import math
import jax
import jax.numpy as jnp
from jax import lax

D = 3072
HEADS = 32
DH = 128
TOKENS = 4096


def levels(stream_key, dims, cuts, smallest, largest):
    factor_of, own = 1.0, jax.random.fold_in(stream_key, 6)
    for dim, shards_of in cuts:
        steps = jnp.exp(jax.random.uniform(jax.random.fold_in(own, dim), (shards_of,), jnp.float32, smallest / len(cuts), largest / len(cuts)))
        factor_of = factor_of * jnp.repeat(steps, dims[dim] // shards_of).reshape([-1 if axis == dim else 1 for axis in range(len(dims))])
    return factor_of


def normal_values(key, extent, width, most, shards=(), kind=jnp.bfloat16):
    array = width * jax.random.normal(key, extent, jnp.float32)
    if shards:
        array = array * levels(key, extent, shards, -0.22, 0.18)
    return jnp.clip(array, -most, most).astype(kind)


def setup_inputs(seed: int = 0) -> dict:
    key_list = jax.random.split(jax.random.key(seed), 6)
    queries = normal_values(key_list[0], (TOKENS, HEADS * DH), 1.0, 6.0, ((0, 16), (1, 2)))
    keys = normal_values(key_list[1], (TOKENS, HEADS * DH), 1.0, 6.0, ((0, 16), (1, 2)))
    values = normal_values(key_list[2], (TOKENS, HEADS * DH), 1.0, 6.0, ((0, 16), (1, 2)))
    gain = jnp.clip(1.0 + 0.18 * jax.random.normal(key_list[3], (HEADS * DH,), jnp.float32), 0.1, 1.9)
    w_out = normal_values(key_list[4], (HEADS * DH, D), (HEADS * DH) ** -0.5, 0.09375, ((0, 2), (1, 16)))
    return {"queries": queries, "keys": keys, "values": values, "gain": gain, "w_out": w_out}


def reference(queries, keys, values, gain, w_out):
    length = queries.shape[0]
    block_rows = math.gcd(length, 512)
    blocks = length // block_rows
    query_all = queries.reshape(blocks, block_rows, HEADS, DH)
    key_all = keys.reshape(blocks, block_rows, HEADS, DH)
    value_all = values.reshape(blocks, block_rows, HEADS, DH)
    causal_mask = jnp.arange(block_rows)[:, None] >= jnp.arange(block_rows)[None, :]
    gain_rows = gain.reshape(HEADS, DH)
    highest = lax.Precision.HIGHEST

    def advance(carried, inputs):
        query_block, key_block, value_block = inputs
        query_f = query_block.astype(jnp.float32)
        key_f = key_block.astype(jnp.float32)
        value_f = value_block.astype(jnp.float32)
        cross = jnp.einsum('thd,hde->the', query_f, carried, precision=highest)
        scores = jnp.einsum('thd,shd->hts', query_f, key_f, precision=highest)
        scores = jnp.where(causal_mask[None], scores, jnp.float32(0.0))
        inner = jnp.einsum('hts,she->the', scores, value_f, precision=highest)
        attn = cross + inner
        carried = carried + jnp.einsum('thd,the->hde', key_f, value_f, precision=highest)
        meansq = lax.optimization_barrier(jnp.mean(attn * attn, axis=-1, keepdims=True))
        normed = (attn * lax.rsqrt(meansq + 1e-06) * gain_rows).astype(jnp.bfloat16)
        normed = normed.reshape(block_rows, HEADS * DH)
        result = jnp.dot(normed, w_out, preferred_element_type=jnp.float32).astype(jnp.bfloat16)
        return (carried, result)
    initial = jnp.zeros((HEADS, DH, DH), jnp.float32)
    _, results = lax.scan(advance, initial, (query_all, key_all, value_all))
    return results.reshape(length, D)
```

```python
import functools

import jax
import jax.numpy as jnp
from jax import lax
from jax.experimental import pallas as pl
from jax.experimental.pallas import tpu as pltpu
from jax.sharding import PartitionSpec as P

DH = 128
GROUP = 4
MESH = pl.DeviceIdType.MESH
F32 = jnp.float32
BF16 = jnp.bfloat16


def dot(a, b, dims=((1,), (0,))):
    return lax.dot_general(a, b, (dims, ((), ())), preferred_element_type=F32)


def head_columns(head):
    return pl.ds(pl.multiple_of(head * DH, DH), DH)


def kernel(
    lines, group, q_ref, k_ref, v_ref, gain_ref, w_ref, out_ref,
    state, state_in, total, before, prior, inner, weights, normed, give, take, ready, landed,
    w_out_sem, w_in_sem, s_out_sem, s_in_sem, t_out_sem, t_in_sem, b_out_sem, b_in_sem,
    n_out_sem, n_in_sem, p_out_sem, p_in_sem, o_out_sem, o_in_sem,
):
    me = lax.axis_index("seq")
    core = lax.axis_index("head")
    line, place = lax.div(me, group), lax.rem(me, group)
    rows, width = q_ref.shape
    part = width // DH // group
    half = rows // 2
    cols = w_ref.shape[1]
    chunk = part * DH

    def at_place(other):
        return (line * group + other, core)

    def at_line(other):
        return (other * group + place, core)

    def peers(mine, count):
        return [lax.rem(mine + step, count) for step in range(1, count)]

    def copy(src, dst, out_sem, in_sem, to):
        return pltpu.make_async_remote_copy(
            src_ref=src, dst_ref=dst, send_sem=out_sem, recv_sem=in_sem, device_id=to, device_id_type=MESH
        )

    near, far = peers(place, group), peers(line, lines)
    twin = (me, 1 - core)
    greeted = [at_place(o) for o in near] + [at_line(o) for o in far] + [twin]
    barrier = pltpu.get_barrier_semaphore()
    for to in greeted:
        pl.semaphore_signal(barrier, inc=1, device_id=to, device_id_type=MESH)
    pl.semaphore_wait(barrier, len(greeted))

    sent = []

    def send(*args):
        started = copy(*args)
        started.start()
        sent.append(started)

    def states_of(owner):
        def body(i, _):
            columns = head_columns(owner * part + i)
            state[owner, i] = dot(k_ref[:, columns], v_ref[:, columns], ((0,), (0,))).astype(BF16)
            return 0

        lax.fori_loop(0, part, body, 0)

    for step, other in enumerate(near):
        states_of(other)
        send(state.at[other], state_in.at[place], s_out_sem.at[step], s_in_sem.at[place], at_place(other))
    for step, other in enumerate(far):
        send(w_ref, weights.at[line], w_out_sem.at[step], w_in_sem.at[line], at_line(other))
    states_of(place)
    state_in[place] = state[place]
    weights[line] = w_ref[...]
    for other in near:
        copy(state.at[other], state_in.at[other], s_out_sem.at[0], s_in_sem.at[other], at_place(other)).wait_recv()
    total[line] = sum(state_in[i].astype(F32) for i in range(group)).astype(BF16)
    for step, other in enumerate(far):
        send(total.at[line], total.at[line], t_out_sem.at[step], t_in_sem.at[line], at_line(other))

    seen = lax.broadcasted_iota(jnp.int32, (rows, rows), 0) >= lax.broadcasted_iota(jnp.int32, (rows, rows), 1)

    def own_tokens(head, _):
        columns = head_columns(head)
        scores = dot(q_ref[:, columns], k_ref[:, columns], ((1,), (1,)))
        scores = jnp.where(seen, scores, 0.0).astype(BF16)
        inner[:, columns] = dot(scores, v_ref[:, columns])
        return 0

    lax.fori_loop(0, width // DH, own_tokens, 0)

    for other in far:
        copy(total.at[other], total.at[other], t_out_sem.at[0], t_in_sem.at[other], at_line(other)).wait_recv()
    running = lax.fori_loop(
        0,
        lines,
        lambda i, acc: acc + jnp.where(i < line, total[i].astype(F32), 0.0),
        jnp.zeros(total.shape[1:], F32),
    )
    for i in range(group):
        before[i] = running.astype(BF16)
        running = running + state_in[i].astype(F32)
    for step, other in enumerate(near):
        send(before.at[other], prior.at[place], b_out_sem.at[step], b_in_sem.at[place], at_place(other))
    prior[place] = before[place]

    def finish(owner, slot):
        def body(i, _):
            columns = head_columns(owner * part + i)
            attn = inner[:, columns] + dot(q_ref[:, columns], prior[owner, i])
            meansq = jnp.mean(attn * attn, axis=-1, keepdims=True)
            result = attn * lax.rsqrt(meansq + 1e-06) * gain_ref[:, columns]
            normed[place, owner, :, head_columns(i)] = result.astype(BF16)
            return 0

        lax.fori_loop(0, part, body, 0)
        for step, other in enumerate(near):
            send(
                normed.at[place, owner], normed.at[place, owner],
                n_out_sem.at[slot, step], n_in_sem.at[place, owner], at_place(other),
            )

    finish(place, 0)
    for slot, other in enumerate(near):
        copy(before.at[other], prior.at[other], b_out_sem.at[0], b_in_sem.at[other], at_place(other)).wait_recv()
        finish(other, slot + 1)

    for other in far:
        copy(w_ref, weights.at[other], w_out_sem.at[0], w_in_sem.at[other], at_line(other)).wait_recv()

    def project(block, first, store):
        picked = pl.ds(pl.multiple_of(first * half, half), half)

        def body(i, _):
            terms = [
                dot(normed[block, j, picked, :], weights[i, j * chunk:(j + 1) * chunk, :]) for j in range(group)
            ]
            store(block, i, sum(terms[1:], terms[0]))
            return 0

        lax.fori_loop(0, lines, body, 0)

    def to_twin(block, i, value):
        give[block, i] = value

    def to_owner(block, i, value):
        ready[block, i] = (value + take[block, i]).astype(BF16)

    blocks = [place] + near
    for step, block in enumerate(blocks):
        if step:
            for j in range(group):
                copy(
                    normed.at[block, j], normed.at[block, j], n_out_sem.at[0, 0], n_in_sem.at[block, j], at_place(block)
                ).wait_recv()
        project(block, 1 - core, to_twin)
        send(give.at[block], take.at[block], p_out_sem.at[step], p_in_sem.at[block], twin)
    for step, block in enumerate(near + [place]):
        copy(give.at[block], take.at[block], p_out_sem.at[0], p_in_sem.at[block], twin).wait_recv()
        project(block, core, to_owner)
        if step < group - 1:
            send(ready.at[block], landed.at[place], o_out_sem.at[step], o_in_sem.at[place], at_place(block))
    landed[place] = ready[place]
    for other in near:
        copy(ready.at[other], landed.at[other], o_out_sem.at[0], o_in_sem.at[other], at_place(other)).wait_recv()
    for i in range(lines):
        for g in range(group):
            start = (i * group + g) * cols
            out_ref[:, start:start + cols] = landed[g, i]
    for started in sent:
        started.wait_send()


def fused(seq_count, queries, keys, values, gain, w_out):
    rows, width = queries.shape
    cols = w_out.shape[1]
    group, lines = GROUP, seq_count // GROUP
    part = width // DH // group
    half = rows // 2
    vmem = pltpu.VMEM
    dma = pltpu.SemaphoreType.DMA
    spec = pl.BlockSpec(memory_space=vmem)
    return pl.pallas_call(
        functools.partial(kernel, lines, group),
        out_shape=jax.ShapeDtypeStruct((half, cols * seq_count), BF16),
        in_specs=[spec] * 5,
        out_specs=spec,
        scratch_shapes=[
            vmem((group, part, DH, DH), BF16),
            vmem((group, part, DH, DH), BF16),
            vmem((lines, part, DH, DH), BF16),
            vmem((group, part, DH, DH), BF16),
            vmem((group, part, DH, DH), BF16),
            vmem((rows, width), F32),
            vmem((lines, width, cols), BF16),
            vmem((group, group, rows, part * DH), BF16),
            vmem((group, lines, half, cols), F32),
            vmem((group, lines, half, cols), F32),
            vmem((group, lines, half, cols), BF16),
            vmem((group, lines, half, cols), BF16),
            dma((lines,)), dma((lines,)),
            dma((group,)), dma((group,)),
            dma((lines,)), dma((lines,)),
            dma((group,)), dma((group,)),
            dma((group, group)), dma((group, group)),
            dma((group,)), dma((group,)),
            dma((group,)), dma((group,)),
        ],
        compiler_params=pltpu.CompilerParams(
            collective_id=0, has_side_effects=True, vmem_limit_bytes=62 * 1024 * 1024
        ),
    )(queries, keys, values, gain.reshape(1, width), w_out)


def solution(mesh):
    return jax.shard_map(
        functools.partial(fused, mesh.shape["seq"]),
        mesh=mesh,
        in_specs=(
            P("seq", "head"),
            P("seq", "head"),
            P("seq", "head"),
            P("head"),
            P("head", "seq"),
        ),
        out_specs=P(("seq", "head"), None),
        check_vma=False,
    )
```

```python
import functools
import math

import jax
import jax.numpy as jnp
from jax import lax
from jax.experimental import pallas as pl
from jax.experimental.pallas import tpu as pltpu
from jax.sharding import PartitionSpec as P

DH = 128
GROUP = 4
EARLY = (0,)
LATER = {0: (1,), 1: (2,), 2: (3,)}
MESH = pl.DeviceIdType.MESH
F32 = jnp.float32
BF16 = jnp.bfloat16


def dot(a, b, dims=((1,), (0,))):
    return lax.dot_general(a, b, (dims, ((), ())), preferred_element_type=F32)


def head_columns(head):
    return pl.ds(pl.multiple_of(head * DH, DH), DH)


def kernel(
    lines, group, q_ref, k_ref, v_ref, gain_ref, w_ref, out_ref,
    state, state_in, total, before, prior, inner, packed, weights, normed, keep, give, take, ready, landed,
    w_out_sem, w_in_sem, s_out_sem, s_in_sem, t_out_sem, t_in_sem, b_out_sem, b_in_sem,
    n_out_sem, n_in_sem, p_out_sem, p_in_sem, o_out_sem, o_in_sem,
):
    me = lax.axis_index("seq")
    core = lax.axis_index("head")
    line, place = lax.div(me, group), lax.rem(me, group)
    rows, width = q_ref.shape
    part = width // DH // group
    half = rows // 2
    fold = width // w_ref.shape[0]
    cols = w_ref.shape[1] // fold
    depth = w_ref.shape[0]
    chunk = part * DH

    def at_place(other):
        return (line * group + other, core)

    def at_line(other):
        return (other * group + place, core)

    def peers(mine, count):
        return [lax.rem(mine + step, count) for step in range(1, count)]

    def copy(src, dst, out_sem, in_sem, to):
        return pltpu.make_async_remote_copy(
            src_ref=src, dst_ref=dst, send_sem=out_sem, recv_sem=in_sem, device_id=to, device_id_type=MESH
        )

    near, far = peers(place, group), peers(line, lines)
    twin = (me, 1 - core)
    greeted = [at_place(o) for o in near] + [at_line(o) for o in far] + [twin]
    barrier = pltpu.get_barrier_semaphore()
    for to in greeted:
        pl.semaphore_signal(barrier, inc=1, device_id=to, device_id_type=MESH)
    pl.semaphore_wait(barrier, len(greeted))

    sent = []

    def send(*args):
        started = copy(*args)
        started.start()
        sent.append(started)

    def states_of(owner):
        def body(i, _):
            columns = head_columns(owner * part + i)
            state[owner, i] = dot(k_ref[:, columns], v_ref[:, columns], ((0,), (0,))).astype(BF16)
            return 0

        lax.fori_loop(0, part, body, 0)

    for step, other in enumerate(near):
        states_of(other)
        send(state.at[other], state_in.at[place], s_out_sem.at[step], s_in_sem.at[place], at_place(other))
    states_of(place)
    state_in[place] = state[place]
    packed[line] = w_ref[...]
    for other in near:
        copy(state.at[other], state_in.at[other], s_out_sem.at[0], s_in_sem.at[other], at_place(other)).wait_recv()
    total[line] = sum(state_in[i].astype(F32) for i in range(group)).astype(BF16)
    for step, other in enumerate(far):
        send(total.at[line], total.at[line], t_out_sem.at[step], t_in_sem.at[line], at_line(other))

    piece = depth // group

    def send_weights(c):
        picked = pl.ds(c * piece, piece)
        for step, other in enumerate(far):
            send(
                w_ref.at[picked, :], packed.at[line, picked, :],
                w_out_sem.at[step, c], w_in_sem.at[line, c], at_line(other),
            )

    for c in EARLY:
        send_weights(c)

    seen = lax.broadcasted_iota(jnp.int32, (rows, rows), 0) >= lax.broadcasted_iota(jnp.int32, (rows, rows), 1)

    def own_tokens(head, _):
        columns = head_columns(head)
        scores = dot(q_ref[:, columns], k_ref[:, columns], ((1,), (1,)))
        scores = jnp.where(seen, scores, 0.0).astype(BF16)
        inner[:, columns] = dot(scores, v_ref[:, columns])
        return 0

    lax.fori_loop(0, width // DH, own_tokens, 0)

    for other in far:
        copy(total.at[other], total.at[other], t_out_sem.at[0], t_in_sem.at[other], at_line(other)).wait_recv()
    running = lax.fori_loop(
        0,
        lines,
        lambda i, acc: acc + jnp.where(i < line, total[i].astype(F32), 0.0),
        jnp.zeros(total.shape[1:], F32),
    )
    for i in range(group):
        before[i] = running.astype(BF16)
        running = running + state_in[i].astype(F32)
    for step, other in enumerate(near):
        send(before.at[other], prior.at[place], b_out_sem.at[step], b_in_sem.at[place], at_place(other))
    prior[place] = before[place]

    def finish(owner, slot):
        def body(i, _):
            columns = head_columns(owner * part + i)
            attn = inner[:, columns] + dot(q_ref[:, columns], prior[owner, i])
            meansq = jnp.mean(attn * attn, axis=-1, keepdims=True)
            result = attn * lax.rsqrt(meansq + 1e-06) * gain_ref[:, columns]
            normed[owner, place, :, head_columns(i)] = result.astype(BF16)
            return 0

        lax.fori_loop(0, part, body, 0)
        for step, other in enumerate(near):
            send(
                normed.at[owner, place], normed.at[owner, place],
                n_out_sem.at[slot, step], n_in_sem.at[place, owner], at_place(other),
            )

        for c in LATER.get(slot, ()):
            send_weights(c)

    finish(place, 0)
    for slot, other in enumerate(near):
        copy(before.at[other], prior.at[other], b_out_sem.at[0], b_in_sem.at[other], at_place(other)).wait_recv()
        finish(other, slot + 1)

    for block in near:
        for j in range(group):
            copy(
                normed.at[j, block], normed.at[j, block], n_out_sem.at[0, 0], n_in_sem.at[block, j], at_place(block)
            ).wait_recv()

    def project(i, first):
        picked = pl.ds(pl.multiple_of(first * half, half), half)
        terms = [
            dot(normed[j, :, picked, :].reshape(group * half, chunk), weights[j * chunk:(j + 1) * chunk, :])
            for j in range(group)
        ]
        return sum(terms[1:], terms[0]).reshape(group, half, cols)

    def collect(i):
        copy(give.at[i], take.at[i], p_out_sem.at[0], p_in_sem.at[i], twin).wait_recv()
        ready[:, i] = (keep[...] + take[i]).astype(BF16)

    order = [line] + far
    for step, i in enumerate(order):
        if step:
            for c in range(group):
                picked = pl.ds(c * piece, piece)
                copy(
                    w_ref.at[picked, :], packed.at[i, picked, :], w_out_sem.at[0, 0], w_in_sem.at[i, c], at_line(i)
                ).wait_recv()
        for f in range(fold):
            weights[f * depth:(f + 1) * depth, :] = packed[i, :, f * cols:(f + 1) * cols]
        give[i] = project(i, 1 - core)
        send(give.at[i], take.at[i], p_out_sem.at[step], p_in_sem.at[i], twin)
        if step:
            collect(order[step - 1])
        keep[...] = project(i, core)
    collect(order[-1])
    for step, other in enumerate(near):
        send(ready.at[other], landed.at[place], o_out_sem.at[step], o_in_sem.at[place], at_place(other))
    landed[place] = ready[place]
    for other in near:
        copy(ready.at[other], landed.at[other], o_out_sem.at[0], o_in_sem.at[other], at_place(other)).wait_recv()
    for i in range(lines):
        for g in range(group):
            start = (i * group + g) * cols
            out_ref[:, start:start + cols] = landed[g, i]
    for started in sent:
        started.wait_send()


def fused(seq_count, queries, keys, values, gain, w_out):
    rows, width = queries.shape
    cols = w_out.shape[1]
    fold = DH // math.gcd(cols, DH)
    w_out = jnp.concatenate(jnp.split(w_out, fold, axis=0), axis=1)
    group, lines = GROUP, seq_count // GROUP
    part = width // DH // group
    half = rows // 2
    vmem = pltpu.VMEM
    dma = pltpu.SemaphoreType.DMA
    spec = pl.BlockSpec(memory_space=vmem)
    return pl.pallas_call(
        functools.partial(kernel, lines, group),
        out_shape=jax.ShapeDtypeStruct((half, cols * seq_count), BF16),
        in_specs=[spec] * 5,
        out_specs=spec,
        scratch_shapes=[
            vmem((group, part, DH, DH), BF16),
            vmem((group, part, DH, DH), BF16),
            vmem((lines, part, DH, DH), BF16),
            vmem((group, part, DH, DH), BF16),
            vmem((group, part, DH, DH), BF16),
            vmem((rows, width), F32),
            vmem((lines,) + w_out.shape, BF16),
            vmem((width, cols), BF16),
            vmem((group, group, rows, part * DH), BF16),
            vmem((group, half, cols), F32),
            vmem((lines, group, half, cols), F32),
            vmem((lines, group, half, cols), F32),
            vmem((group, lines, half, cols), BF16),
            vmem((group, lines, half, cols), BF16),
            dma((lines, group)), dma((lines, group)),
            dma((group,)), dma((group,)),
            dma((lines,)), dma((lines,)),
            dma((group,)), dma((group,)),
            dma((group, group)), dma((group, group)),
            dma((lines,)), dma((lines,)),
            dma((group,)), dma((group,)),
        ],
        compiler_params=pltpu.CompilerParams(
            collective_id=0, has_side_effects=True, vmem_limit_bytes=62 * 1024 * 1024
        ),
    )(queries, keys, values, gain.reshape(1, width), w_out)


def solution(mesh):
    return jax.shard_map(
        functools.partial(fused, mesh.shape["seq"]),
        mesh=mesh,
        in_specs=(
            P("seq", "head"),
            P("seq", "head"),
            P("seq", "head"),
            P("head"),
            P("head", "seq"),
        ),
        out_specs=P(("seq", "head"), None),
        check_vma=False,
    )
```

```python
import functools
import math

import jax
import jax.numpy as jnp
from jax import lax
from jax.experimental import pallas as pl
from jax.experimental.pallas import tpu as pltpu
from jax.sharding import PartitionSpec as P

DH = 128
GROUP = 4
EARLY = (0,)
LATER = {0: (1,), 1: (2,), 2: (3,)}
MESH = pl.DeviceIdType.MESH
F32 = jnp.float32
BF16 = jnp.bfloat16


def dot(a, b, dims=((1,), (0,))):
    return lax.dot_general(a, b, (dims, ((), ())), preferred_element_type=F32)


def head_columns(head):
    return pl.ds(pl.multiple_of(head * DH, DH), DH)


def kernel(
    lines, group, q_ref, k_ref, v_ref, gain_ref, w_ref, out_ref,
    state, state_in, total, before, prior, inner, packed, weights, normed, keep, give, take, ready, landed,
    w_out_sem, w_in_sem, s_out_sem, s_in_sem, t_out_sem, t_in_sem, b_out_sem, b_in_sem,
    n_out_sem, n_in_sem, p_out_sem, p_in_sem, o_out_sem, o_in_sem,
):
    me = lax.axis_index("seq")
    core = lax.axis_index("head")
    line, place = lax.div(me, group), lax.rem(me, group)
    rows, width = q_ref.shape
    part = width // DH // group
    half = rows // 2
    fold = width // w_ref.shape[0]
    cols = w_ref.shape[1] // fold
    depth = w_ref.shape[0]
    chunk = part * DH

    def at_place(other):
        return (line * group + other, core)

    def at_line(other):
        return (other * group + place, core)

    def peers(mine, count):
        return [lax.rem(mine + step, count) for step in range(1, count)]

    def copy(src, dst, out_sem, in_sem, to):
        return pltpu.make_async_remote_copy(
            src_ref=src, dst_ref=dst, send_sem=out_sem, recv_sem=in_sem, device_id=to, device_id_type=MESH
        )

    near, far = peers(place, group), peers(line, lines)
    twin = (me, 1 - core)
    greeted = [at_place(o) for o in near] + [at_line(o) for o in far] + [twin]
    barrier = pltpu.get_barrier_semaphore()
    for to in greeted:
        pl.semaphore_signal(barrier, inc=1, device_id=to, device_id_type=MESH)
    pl.semaphore_wait(barrier, len(greeted))

    sent = []

    def send(*args):
        started = copy(*args)
        started.start()
        sent.append(started)

    def states_of(owner):
        def body(i, _):
            columns = head_columns(owner * part + i)
            state[owner, i] = dot(k_ref[:, columns], v_ref[:, columns], ((0,), (0,))).astype(BF16)
            return 0

        lax.fori_loop(0, part, body, 0, unroll=True)

    for step, other in enumerate(near):
        states_of(other)
        send(state.at[other], state_in.at[place], s_out_sem.at[step], s_in_sem.at[place], at_place(other))
    states_of(place)
    state_in[place] = state[place]
    packed[line] = w_ref[...]
    for other in near:
        copy(state.at[other], state_in.at[other], s_out_sem.at[0], s_in_sem.at[other], at_place(other)).wait_recv()
    total[line] = sum(state_in[i].astype(F32) for i in range(group)).astype(BF16)
    for step, other in enumerate(far):
        send(total.at[line], total.at[line], t_out_sem.at[step], t_in_sem.at[line], at_line(other))

    piece = depth // group

    def send_weights(c):
        picked = pl.ds(c * piece, piece)
        for step, other in enumerate(far):
            send(
                w_ref.at[picked, :], packed.at[line, picked, :],
                w_out_sem.at[step, c], w_in_sem.at[line, c], at_line(other),
            )

    for c in EARLY:
        send_weights(c)

    seen = lax.broadcasted_iota(jnp.int32, (rows, rows), 0) >= lax.broadcasted_iota(jnp.int32, (rows, rows), 1)

    def own_tokens(head, _):
        columns = head_columns(head)
        scores = dot(q_ref[:, columns], k_ref[:, columns], ((1,), (1,)))
        scores = jnp.where(seen, scores, 0.0).astype(BF16)
        inner[:, columns] = dot(scores, v_ref[:, columns])
        return 0

    def own_share(share, _):
        for i in range(part):
            own_tokens(share * part + i, 0)
        return 0

    lax.fori_loop(0, group, own_share, 0)

    for other in far:
        copy(total.at[other], total.at[other], t_out_sem.at[0], t_in_sem.at[other], at_line(other)).wait_recv()
    running = lax.fori_loop(
        0,
        lines,
        lambda i, acc: acc + jnp.where(i < line, total[i].astype(F32), 0.0),
        jnp.zeros(total.shape[1:], F32),
    )
    for i in range(group):
        before[i] = running.astype(BF16)
        running = running + state_in[i].astype(F32)
    for step, other in enumerate(near):
        send(before.at[other], prior.at[place], b_out_sem.at[step], b_in_sem.at[place], at_place(other))
    prior[place] = before[place]

    def finish(owner, slot):
        def body(i, _):
            columns = head_columns(owner * part + i)
            attn = inner[:, columns] + dot(q_ref[:, columns], prior[owner, i])
            meansq = jnp.mean(attn * attn, axis=-1, keepdims=True)
            result = attn * lax.rsqrt(meansq + 1e-06) * gain_ref[:, columns]
            normed[owner, place, :, head_columns(i)] = result.astype(BF16)
            return 0

        lax.fori_loop(0, part, body, 0, unroll=True)
        for step, other in enumerate(near):
            send(
                normed.at[owner, place], normed.at[owner, place],
                n_out_sem.at[slot, step], n_in_sem.at[place, owner], at_place(other),
            )

        for c in LATER.get(slot, ()):
            send_weights(c)

    finish(place, 0)
    for slot, other in enumerate(near):
        copy(before.at[other], prior.at[other], b_out_sem.at[0], b_in_sem.at[other], at_place(other)).wait_recv()
        finish(other, slot + 1)

    for block in near:
        for j in range(group):
            copy(
                normed.at[j, block], normed.at[j, block], n_out_sem.at[0, 0], n_in_sem.at[block, j], at_place(block)
            ).wait_recv()

    def project(i, first):
        picked = pl.ds(pl.multiple_of(first * half, half), half)
        terms = [
            dot(normed[j, :, picked, :].reshape(group * half, chunk), weights[j * chunk:(j + 1) * chunk, :])
            for j in range(group)
        ]
        return sum(terms[1:], terms[0]).reshape(group, half, cols)

    def collect(i):
        copy(give.at[i], take.at[i], p_out_sem.at[0], p_in_sem.at[i], twin).wait_recv()
        ready[:, i] = (keep[...] + take[i]).astype(BF16)

    order = [line] + far
    for step, i in enumerate(order):
        if step:
            for c in range(group):
                picked = pl.ds(c * piece, piece)
                copy(
                    w_ref.at[picked, :], packed.at[i, picked, :], w_out_sem.at[0, 0], w_in_sem.at[i, c], at_line(i)
                ).wait_recv()
        for f in range(fold):
            weights[f * depth:(f + 1) * depth, :] = packed[i, :, f * cols:(f + 1) * cols]
        give[i] = project(i, 1 - core)
        send(give.at[i], take.at[i], p_out_sem.at[step], p_in_sem.at[i], twin)
        if step:
            collect(order[step - 1])
        keep[...] = project(i, core)
    collect(order[-1])
    for step, other in enumerate(near):
        send(ready.at[other], landed.at[place], o_out_sem.at[step], o_in_sem.at[place], at_place(other))
    landed[place] = ready[place]
    for other in near:
        copy(ready.at[other], landed.at[other], o_out_sem.at[0], o_in_sem.at[other], at_place(other)).wait_recv()
    for i in range(lines):
        for g in range(group):
            start = (i * group + g) * cols
            out_ref[:, start:start + cols] = landed[g, i]
    for started in sent:
        started.wait_send()


def fused(seq_count, queries, keys, values, gain, w_out):
    rows, width = queries.shape
    cols = w_out.shape[1]
    fold = DH // math.gcd(cols, DH)
    w_out = jnp.concatenate(jnp.split(w_out, fold, axis=0), axis=1)
    group, lines = GROUP, seq_count // GROUP
    part = width // DH // group
    half = rows // 2
    vmem = pltpu.VMEM
    dma = pltpu.SemaphoreType.DMA
    spec = pl.BlockSpec(memory_space=vmem)
    return pl.pallas_call(
        functools.partial(kernel, lines, group),
        out_shape=jax.ShapeDtypeStruct((half, cols * seq_count), BF16),
        in_specs=[spec] * 5,
        out_specs=spec,
        scratch_shapes=[
            vmem((group, part, DH, DH), BF16),
            vmem((group, part, DH, DH), BF16),
            vmem((lines, part, DH, DH), BF16),
            vmem((group, part, DH, DH), BF16),
            vmem((group, part, DH, DH), BF16),
            vmem((rows, width), F32),
            vmem((lines,) + w_out.shape, BF16),
            vmem((width, cols), BF16),
            vmem((group, group, rows, part * DH), BF16),
            vmem((group, half, cols), F32),
            vmem((lines, group, half, cols), F32),
            vmem((lines, group, half, cols), F32),
            vmem((group, lines, half, cols), BF16),
            vmem((group, lines, half, cols), BF16),
            dma((lines, group)), dma((lines, group)),
            dma((group,)), dma((group,)),
            dma((lines,)), dma((lines,)),
            dma((group,)), dma((group,)),
            dma((group, group)), dma((group, group)),
            dma((lines,)), dma((lines,)),
            dma((group,)), dma((group,)),
        ],
        compiler_params=pltpu.CompilerParams(
            collective_id=0, has_side_effects=True, vmem_limit_bytes=62 * 1024 * 1024
        ),
    )(queries, keys, values, gain.reshape(1, width), w_out)


def solution(mesh):
    return jax.shard_map(
        functools.partial(fused, mesh.shape["seq"]),
        mesh=mesh,
        in_specs=(
            P("seq", "head"),
            P("seq", "head"),
            P("seq", "head"),
            P("head"),
            P("head", "seq"),
        ),
        out_specs=P(("seq", "head"), None),
        check_vma=False,
    )
```
